512 devices in a mesh: band: 16 (over z_lo, x), head: 8 (over z_hi, core), member: 4 (over y).
Axes of the slice: x: 4, y: 4, z: 16 (z_hi: 4, z_lo: 4; z = z_hi * 4 + z_lo), core: 2. Of those that a mesh axis runs over, the one named last changes fastest.
Arguments:
- tokens: bfloat16 [229376, 1024], P(('member', 'band')), parts along dimension 0, may hold values from -48 to 48
- ln_gain: float32 [1024], replicated, may hold values from 0.1 to 1.9
- qkv_weight: bfloat16 [1024, 3, 1024], P(None, None, 'head'), may hold values from -0.1875 to 0.1875
- qk_gain: float32 [2, 16, 64], P(None, 'head'), may hold values from 0.1 to 1.9
- out_weight: bfloat16 [1024, 1024], replicated, may hold values from -0.1875 to 0.1875
- key_start: int32 [448], P('band'), may hold values from 0 to 446, as said below
- key_count: int32 [448], P('band'), may hold values from 2 to 15, as said below
Outputs:
- updated: bfloat16 [229376, 1024], P(('member', 'band', 'head')), parts along dimension 0
The draws below stay inside these ranges and needn't reach their ends.
There are 4 independent parts, one for each index of `member`. The reference program is written for one: setup_inputs(seed, part) draws one part's arguments, and reference() takes and returns one part's arrays. A program takes and returns all parts, laid end to end along the dimension named above; an argument that names none is the same for every part. Nothing has to cross between parts.
Inputs may be any that keep to these rules, and one draw needn't show every extreme that they name: Query block b's window begins at key block key_start[b], where b - 7 <= key_start[b] <= b. The window of query block b ends at key block key_start[b] + key_count[b] - 1, which is at least b, at most b + 7, and at most the last block.
All inputs are finite; a program needn't handle non-finite values.
Results may differ from the reference program's by a relative error of at most 0.0034.
Values may be sent and summed in bfloat16 or wider, within the bound.
A program may use at most 128 MiB of HBM per device.

```python
import jax
import jax.numpy as jnp
from jax import lax

D = 1024
HEADS = 16
HD = 64
BLOCK = 128
REACH = 7
BLK_DEV = 28
NBLK = 448
TOKENS = 57344
N_BAND = 16


def window_reach(key):
    count_blocks = BLK_DEV * N_BAND
    position = jnp.arange(count_blocks, dtype=jnp.int32)
    distance = jnp.abs(2 * position + 1 - count_blocks)
    base_reach = 1 + (REACH - 1) * (count_blocks - distance) // count_blocks
    jitter = jax.random.randint(key, (2, count_blocks), -1, 2, dtype=jnp.int32)
    reach = jnp.clip(base_reach[None, :] + jitter, 1, REACH)
    reach = jnp.where(position[None, :] == count_blocks // 2, REACH, reach)
    edges = (position == 0) | (position == count_blocks - 1)
    reach = jnp.where(edges[None, :], 1, reach)
    first = jnp.maximum(position - reach[0], 0)
    last = jnp.minimum(position + reach[1], count_blocks - 1)
    return (first.astype(jnp.int32), (last - first + 1).astype(jnp.int32))


def draw_key_start(key, part):
    return window_reach(jax.random.fold_in(key, 5))[0]


def draw_key_count(key, part):
    return window_reach(jax.random.fold_in(key, 5))[1]


def draw_tokens(key, part):
    key = jax.random.fold_in(key, 11)
    first_key = jax.random.fold_in(key, 0)
    values = jnp.clip(jax.random.normal(first_key, (TOKENS, D), jnp.float32), -6.0, 6.0)
    return values.astype(jnp.bfloat16)


def level_of(stream_key, extent, cuts, low, top_value):
    level, own = 1.0, jax.random.fold_in(stream_key, 6)
    for dim, shards_of in cuts:
        heights = jnp.exp(jax.random.uniform(jax.random.fold_in(own, dim), (shards_of,), jnp.float32, low / len(cuts), top_value / len(cuts)))
        level = level * jnp.repeat(heights, extent[dim] // shards_of).reshape([-1 if axis == dim else 1 for axis in range(len(extent))])
    return level


def noise(key, dims, scale, limit, shards=(), kind=jnp.bfloat16):
    result = scale * jax.random.normal(key, dims, jnp.float32)
    if shards:
        result = result * level_of(key, dims, shards, -0.22, 0.18)
    return jnp.clip(result, -limit, limit).astype(kind)


def setup_inputs(seed: int = 0, part: int = 0) -> dict:
    keys = jax.random.split(jax.random.key(seed), 8)
    part_splits = jax.random.split(jax.random.fold_in(keys[7], part), 8)
    return {
        "tokens": draw_tokens(jax.random.fold_in(jax.random.fold_in(keys[7], part), 71), part),
        "ln_gain": jnp.clip(1.0 + 0.18 * jax.random.normal(keys[1], (D,), jnp.float32), 0.1, 1.9),
        "qkv_weight": noise(keys[2], (D, 3, D), D ** -0.5, 0.1875, ((2, 8),)),
        "qk_gain": jnp.clip(1.0 + 0.18 * jax.random.normal(keys[3], (2, HEADS, HD), jnp.float32), 0.1, 1.9),
        "out_weight": noise(keys[4], (D, D), D ** -0.5, 0.1875),
        "key_start": draw_key_start(jax.random.fold_in(keys[7], 71), part),
        "key_count": draw_key_count(jax.random.fold_in(keys[7], 71), part),
    }


def layer_normed(tokens, ln_gain):
    values = tokens.astype(jnp.float32)
    center = lax.optimization_barrier(jnp.mean(values, axis=-1, keepdims=True))
    spread = lax.optimization_barrier(jnp.mean(jnp.square(values - center), axis=-1, keepdims=True))
    return ((values - center) * lax.rsqrt(spread + 1e-05) * ln_gain).astype(jnp.bfloat16)

def head_normed(values, gains):
    inverse = lax.rsqrt(lax.optimization_barrier(jnp.mean(jnp.square(values), axis=-1, keepdims=True)) + 1e-06)
    return (values * inverse * gains).astype(jnp.bfloat16)

def reference(tokens, ln_gain, qkv_weight, qk_gain, out_weight, key_start, key_count):
    normed = layer_normed(tokens, ln_gain)
    projected = jnp.dot(normed, qkv_weight.reshape(D, 3 * D), preferred_element_type=jnp.float32)
    projected = projected.reshape(TOKENS, 3, HEADS, HD)
    queries = head_normed(projected[:, 0], qk_gain[0])
    keys_all = head_normed(projected[:, 1], qk_gain[1])
    values_all = projected[:, 2].astype(jnp.bfloat16)
    span = (2 * REACH + 1) * BLOCK
    padding = jnp.zeros((span, HEADS, HD), jnp.bfloat16)
    keys_pad = jnp.concatenate([keys_all, padding], 0)
    values_pad = jnp.concatenate([values_all, padding], 0)
    scale = HD ** (-0.5)

    def one_block(index):
        q_first = (index * BLOCK).astype(jnp.int32)
        q_block = lax.dynamic_slice_in_dim(queries, q_first, BLOCK, 0).astype(jnp.float32)
        begin = (key_start[index] * BLOCK).astype(jnp.int32)
        k_window = lax.dynamic_slice_in_dim(keys_pad, begin, span, 0).astype(jnp.float32)
        v_window = lax.dynamic_slice_in_dim(values_pad, begin, span, 0).astype(jnp.float32)
        scores = jnp.einsum('ihd,jhd->hij', q_block, k_window) * scale
        live = (jnp.arange(span, dtype=jnp.int32) < key_count[index] * BLOCK).astype(jnp.float32)
        weights = jnp.exp(scores) * live
        total = lax.optimization_barrier(jnp.sum(weights, axis=-1))
        rounded = lax.optimization_barrier(weights.astype(jnp.bfloat16)).astype(jnp.float32)
        mixed = jnp.einsum('hij,jhd->ihd', rounded, v_window)
        return (mixed / jnp.transpose(total)[:, :, None]).astype(jnp.bfloat16)
    blocks = lax.map(one_block, jnp.arange(NBLK, dtype=jnp.int32))
    attended = blocks.reshape(TOKENS, D)
    mixed_out = jnp.dot(attended, out_weight, preferred_element_type=jnp.float32)
    return (tokens.astype(jnp.float32) + mixed_out).astype(jnp.bfloat16)
```

```python
import functools

import jax
import jax.numpy as jnp
from jax import lax
from jax.experimental import pallas as pl
from jax.experimental.pallas import tpu as pltpu
from jax.sharding import PartitionSpec as P

BLOCK = 128
REACH = 7
SPAN = (2 * REACH + 1) * BLOCK
CHUNK = 256
LOG2E = 1.4426950408889634
DEAD = -30000.0
F32 = jnp.float32
BF16 = jnp.bfloat16


def pair_ones():
    row = lax.broadcasted_iota(jnp.int32, (256, 128), 0)
    col = lax.broadcasted_iota(jnp.int32, (256, 128), 1)
    return (((row // 64) % 2) == (col // 64)).astype(BF16)


def layer_normed(values, gain):
    center = jnp.mean(values, axis=-1, keepdims=True)
    shifted = values - center
    spread = jnp.mean(jnp.square(shifted), axis=-1, keepdims=True)
    return (shifted * lax.rsqrt(spread + 1e-05) * gain).astype(BF16)


def head_normed(raw, gain, ones):
    square = raw * raw
    high = square.astype(BF16)
    low = (square - high.astype(F32)).astype(BF16)
    total = jnp.dot(jnp.concatenate([high, low], 1), ones, preferred_element_type=F32)
    return (raw * lax.rsqrt(total * (1.0 / 64.0) + 1e-06) * gain).astype(BF16)


def project(tok_ref, ln_ref, w_ref, gain_ref, q_ref, kv_ref):
    normed = layer_normed(tok_ref[...].astype(F32), ln_ref[...])
    raw = jnp.dot(normed, w_ref[...], preferred_element_type=F32)
    ones = pair_ones()
    q_ref[...] = head_normed(raw[:, :128], gain_ref[0:1, :] * (LOG2E / 8.0), ones)
    kv_ref[:, :128] = head_normed(raw[:, 128:256], gain_ref[1:2, :], ones)
    kv_ref[:, 128:] = raw[:, 256:].astype(BF16)


def attend(q_ref, left_ref, mid_ref, right_ref, bias_ref, out_ref, ka, va):
    width = REACH * BLOCK
    rows = mid_ref.shape[0]
    for ref, first, count in ((left_ref, 0, width), (mid_ref, width, rows), (right_ref, width + rows, width)):
        ka[pl.ds(first, count), :128] = ref[:, :128]
        va[pl.ds(first, count), :128] = ref[:, 128:]
    total = rows + 2 * width
    block_id = lax.broadcasted_iota(jnp.int32, (total, 128), 0) // BLOCK
    ka[:, 128:] = (block_id == lax.broadcasted_iota(jnp.int32, (total, 128), 1)).astype(BF16)
    va[:, 128:] = jnp.ones((total, 128), BF16)
    lane = lax.broadcasted_iota(jnp.int32, (BLOCK, 128), 1)

    def one_block(i, carry):
        first = pl.multiple_of(i * BLOCK, BLOCK)
        q = q_ref[pl.ds(first, BLOCK), :]
        zero = jnp.zeros_like(q)
        bias = jnp.broadcast_to(bias_ref[pl.ds(i, 1), :], (BLOCK, 128)).astype(BF16)
        both = jnp.concatenate(
            [
                jnp.concatenate([jnp.where(lane < 64, q, zero), bias], 1),
                jnp.concatenate([jnp.where(lane < 64, zero, q), bias], 1),
            ],
            0,
        )
        acc = None
        for j in range(0, SPAN, CHUNK):
            count = min(CHUNK, SPAN - j)
            scores = lax.dot_general(
                both, ka[pl.ds(first + j, count), :], (((1,), (1,)), ((), ())), preferred_element_type=F32
            )
            weights = jnp.exp2(scores).astype(BF16)
            part = jnp.dot(weights, va[pl.ds(first + j, count), :], preferred_element_type=F32)
            acc = part if acc is None else acc + part
        mixed = acc[:, :128] * (1.0 / acc[:, 128:])
        out_ref[pl.ds(first, BLOCK), :] = jnp.where(lane < 64, mixed[:BLOCK], mixed[BLOCK:]).astype(BF16)
        return carry

    lax.fori_loop(0, rows // BLOCK, one_block, 0)


def on_device(tokens, ln_gain, qkv_weight, qk_gain, out_weight, key_start, key_count):
    rows, features = tokens.shape
    columns = qk_gain.shape[1] * qk_gain.shape[2]
    num_blocks = rows // BLOCK
    width = REACH * BLOCK
    step = 448
    weight = qkv_weight.reshape(features, 3 * columns)
    whole = pl.BlockSpec(memory_space=pltpu.VMEM)
    queries, kv = pl.pallas_call(
        project,
        grid=(rows // step,),
        out_shape=(
            jax.ShapeDtypeStruct((rows, columns), BF16),
            jax.ShapeDtypeStruct((rows, 2 * columns), BF16),
        ),
        in_specs=[pl.BlockSpec((step, features), lambda i: (i, 0)), whole, whole, whole],
        out_specs=(
            pl.BlockSpec((step, columns), lambda i: (i, 0)),
            pl.BlockSpec((step, 2 * columns), lambda i: (i, 0)),
        ),
        compiler_params=pltpu.CompilerParams(vmem_limit_bytes=40 << 20),
        name="project",
    )(tokens, ln_gain.reshape(1, features), weight, qk_gain.reshape(2, columns))
    band = lax.axis_size("band")
    left = lax.ppermute(kv[rows - width :], "band", [(i, i + 1) for i in range(band - 1)])
    right = lax.ppermute(kv[:width], "band", [(i + 1, i) for i in range(band - 1)])
    first = (key_start - (lax.axis_index("band") * num_blocks - REACH))[:, None]
    block = jnp.arange(128, dtype=jnp.int32)[None, :]
    live = (block >= first) & (block < first + key_count[:, None])
    bias = jnp.where(live, 0.0, DEAD).astype(F32)
    attended = pl.pallas_call(
        attend,
        out_shape=jax.ShapeDtypeStruct((rows, columns), BF16),
        in_specs=[whole] * 5,
        out_specs=whole,
        scratch_shapes=[
            pltpu.VMEM((rows + 2 * width, 256), BF16),
            pltpu.VMEM((rows + 2 * width, 256), BF16),
        ],
        compiler_params=pltpu.CompilerParams(vmem_limit_bytes=40 << 20),
        name="attend",
    )(queries, left, kv, right, bias)
    share = rows // lax.axis_size("head")
    head_pos = lax.axis_index("head")
    residual_rows = lax.dynamic_slice_in_dim(tokens, head_pos * share, share, 0).astype(F32)
    all_heads = lax.all_to_all(attended, "head", split_axis=0, concat_axis=1, tiled=True)
    summed = jnp.dot(all_heads, out_weight, preferred_element_type=F32)
    return (residual_rows + summed).astype(BF16)


def solution(mesh):
    placed = (
        P(("member", "band"), None),
        P(),
        P(None, None, "head"),
        P(None, "head", None),
        P(),
        P("band"),
        P("band"),
    )
    return jax.shard_map(
        on_device,
        mesh=mesh,
        in_specs=placed,
        out_specs=P(("member", "band", "head"), None),
        check_vma=False,
    )
```

```python
import jax
import jax.numpy as jnp
from jax import lax
from jax.experimental import pallas as pl
from jax.experimental.pallas import tpu as pltpu
from jax.sharding import PartitionSpec as P

BLOCK = 128
REACH = 7
WIDE = REACH * BLOCK
SPAN = (2 * REACH + 1) * BLOCK
HALF = WIDE // 2
STEP = 448
CHUNK = 256
LOG2E = 1.4426950408889634
DEAD = -30000.0
F32 = jnp.float32
BF16 = jnp.bfloat16
MESH = pl.DeviceIdType.MESH


def pair_ones():
    row = lax.broadcasted_iota(jnp.int32, (256, 128), 0)
    col = lax.broadcasted_iota(jnp.int32, (256, 128), 1)
    return (((row // 64) % 2) == (col // 64)).astype(BF16)


def layer_normed(values, gain):
    center = jnp.mean(values, axis=-1, keepdims=True)
    shifted = values - center
    spread = jnp.mean(jnp.square(shifted), axis=-1, keepdims=True)
    return (shifted * lax.rsqrt(spread + 1e-05) * gain).astype(BF16)


def head_normed(raw, gain, ones):
    square = raw * raw
    high = square.astype(BF16)
    low = (square - high.astype(F32)).astype(BF16)
    total = jnp.dot(jnp.concatenate([high, low], 1), ones, preferred_element_type=F32)
    return (raw * lax.rsqrt(total * (1.0 / 64.0) + 1e-06) * gain).astype(BF16)


def rows_at(first, count):
    return pl.ds(pl.multiple_of(first, 64), count)


def attend_block(q, bias, kv, first, lane):
    zero = jnp.zeros_like(q)
    bias = jnp.broadcast_to(bias, (BLOCK, 128)).astype(BF16)
    both = jnp.concatenate(
        [
            jnp.concatenate([jnp.where(lane < 64, q, zero), bias], 1),
            jnp.concatenate([jnp.where(lane < 64, zero, q), bias], 1),
        ],
        0,
    )
    acc = None
    for j in range(0, SPAN, CHUNK):
        count = min(CHUNK, SPAN - j)
        marks = [(lane == (j // BLOCK + m)).astype(BF16) for m in range(count // BLOCK)]
        keys = jnp.concatenate([kv[rows_at(first + j, count), :128], jnp.concatenate(marks, 0)], 1)
        values = jnp.concatenate([kv[rows_at(first + j, count), 128:], jnp.ones((count, 128), BF16)], 1)
        scores = lax.dot_general(both, keys, (((1,), (1,)), ((), ())), preferred_element_type=F32)
        part = jnp.dot(jnp.exp2(scores).astype(BF16), values, preferred_element_type=F32)
        acc = part if acc is None else acc + part
    mixed = acc[:, :128] * (1.0 / acc[:, 128:])
    return jnp.where(lane < 64, mixed[:BLOCK], mixed[BLOCK:]).astype(BF16)


def layer(
    tok, ln, w_hbm, gain, ow_hbm, bias, out,
    xv, w, ow, kv, qs, att, rcv, res,
    in_sem, w_sem, halo_send, halo_recv, give_send, give_recv, keep_sem,
):
    band = lax.axis_index("band")
    head = lax.axis_index("head")
    bands = 16
    t = head // 2
    c = head % 2
    t_op = (t + 2) % 4
    t_a = 1 + t % 2
    t_b = 3 * ((t + 1) % 2)

    order = (3, 0, 1, 2)
    loads = {}
    for ch in order:
        loads[ch] = pltpu.make_async_copy(
            tok.at[pl.ds(ch * WIDE, WIDE), :], xv.at[pl.ds(ch * WIDE, WIDE), :], in_sem.at[ch]
        )
    loads[3].start()
    load_w = pltpu.make_async_copy(w_hbm, w, w_sem.at[0])
    load_w.start()
    for ch in order[1:]:
        loads[ch].start()
    load_ow = pltpu.make_async_copy(ow_hbm, ow, w_sem.at[1])
    load_ow.start()
    load_res = pltpu.make_async_copy(tok.at[rows_at(t * WIDE + c * HALF, HALF), :], res, w_sem.at[2])
    load_res.start()

    barrier = pltpu.get_barrier_semaphore()
    for d in range(1, 8):
        pl.semaphore_signal(barrier, inc=1, device_id={"head": (head + d) % 8}, device_id_type=MESH)

    for d in (1, bands - 1):
        pl.semaphore_signal(barrier, inc=1, device_id={"band": (band + d) % bands}, device_id_type=MESH)

    @pl.when(band == 0)
    def _():
        kv[pl.ds(0, WIDE), :] = jnp.zeros((WIDE, 256), BF16)

    @pl.when(band == bands - 1)
    def _():
        kv[pl.ds(5 * WIDE, WIDE), :] = jnp.zeros((WIDE, 256), BF16)

    ones = pair_ones()
    q_gain = gain[0:1, :] * (LOG2E / 8.0)
    k_gain = gain[1:2, :]

    def project(ch):
        def step(s, carry):
            first = ch * WIDE + s * STEP
            normed = layer_normed(xv[rows_at(first, STEP), :].astype(F32), ln[...])
            raw = jnp.dot(normed, w[...], preferred_element_type=F32)
            qs[rows_at(first, STEP), :] = head_normed(raw[:, :128], q_gain, ones)
            kv[rows_at(WIDE + first, STEP), :128] = head_normed(raw[:, 128:256], k_gain, ones)
            kv[rows_at(WIDE + first, STEP), 128:] = raw[:, 256:].astype(BF16)
            return carry

        lax.fori_loop(0, WIDE // STEP, step, 0)

    def halo(side):
        return pltpu.make_async_remote_copy(
            src_ref=kv.at[pl.ds((4 - 3 * side) * WIDE, WIDE), :],
            dst_ref=kv.at[pl.ds(5 * side * WIDE, WIDE), :],
            send_sem=halo_send.at[side],
            recv_sem=halo_recv.at[side],
            device_id={"band": band + 1 - 2 * side},
            device_id_type=MESH,
        )

    loads[3].wait()
    load_w.wait()
    project(3)
    pl.semaphore_wait(barrier, 9)

    @pl.when(band < bands - 1)
    def _():
        halo(0).start()

    loads[0].wait()
    project(0)

    @pl.when(band > 0)
    def _():
        halo(1).start()

    for ch in (1, 2):
        loads[ch].wait()
        project(ch)

    lane = lax.broadcasted_iota(jnp.int32, (BLOCK, 128), 1)
    column = pl.multiple_of(head * 128, 128)

    def give(unit, part, chip, core, slot):
        return pltpu.make_async_remote_copy(
            src_ref=att.at[pl.ds(unit * WIDE + part * HALF, HALF), :],
            dst_ref=rcv.at[:, pl.ds(column, 128)],
            send_sem=give_send.at[slot],
            recv_sem=give_recv.at[head],
            device_id={"head": chip * 2 + core},
            device_id_type=MESH,
        )

    chips = (t_a, t_op, t_b, t)

    def block(unit, i):
        first = chips[unit] * WIDE + i * BLOCK
        att[pl.ds(unit * WIDE + i * BLOCK, BLOCK), :] = attend_block(
            qs[rows_at(first, BLOCK), :], bias[pl.ds(chips[unit] * REACH + i, 1), :], kv, first, lane
        )

    for i in range(7):
        block(0, i)
        if i == 3:
            give(0, 0, t_a, 0, 0).start()
    give(0, 1, t_a, 1, 1).start()

    @pl.when(band > 0)
    def _():
        halo(0).wait_recv()

    @pl.when(band < bands - 1)
    def _():
        halo(1).wait_recv()

    for part in range(2):
        for unit in (1, 2):
            for i in range(4 * part, 4 + 3 * part):
                block(unit, i)
            give(unit, part, chips[unit], part, 2 * unit + part).start()
    for i in range(7):
        block(3, i)
        if i == 3:

            @pl.when(c == 1)
            def _():
                give(3, 0, t, 0, 6).start()

    keep = pltpu.make_async_copy(
        att.at[pl.ds(pl.multiple_of(3 * WIDE + c * HALF, 64), HALF), :], rcv.at[:, pl.ds(column, 128)], keep_sem
    )
    keep.start()

    @pl.when(c == 0)
    def _():
        give(3, 1, t, 1, 6).start()

    load_ow.wait()
    load_res.wait()
    keep.wait()
    for d in range(1, 8):
        peer = (head + d) % 8
        pltpu.make_async_remote_copy(
            src_ref=att.at[pl.ds(0, HALF), :],
            dst_ref=rcv.at[:, pl.ds(pl.multiple_of(peer * 128, 128), 128)],
            send_sem=give_send.at[0],
            recv_sem=give_recv.at[peer],
            device_id={"head": peer},
            device_id_type=MESH,
        ).wait_recv()
    for r in range(0, HALF, 224):
        summed = jnp.dot(rcv[pl.ds(r, 224), :], ow[...], preferred_element_type=F32)
        out[pl.ds(r, 224), :] = (res[pl.ds(r, 224), :].astype(F32) + summed).astype(BF16)
    for slot, unit in enumerate((0, 0, 1, 1, 2, 2)):
        give(unit, slot % 2, chips[unit], slot % 2, slot).wait_send()

    @pl.when(c == 1)
    def _():
        give(3, 0, t, 0, 6).wait_send()

    @pl.when(c == 0)
    def _():
        give(3, 1, t, 1, 6).wait_send()

    @pl.when(band < bands - 1)
    def _():
        halo(0).wait_send()

    @pl.when(band > 0)
    def _():
        halo(1).wait_send()


def on_device(tokens, ln_gain, qkv_weight, qk_gain, out_weight, key_start, key_count):
    rows, features = tokens.shape
    columns = qk_gain.shape[1] * qk_gain.shape[2]
    num_blocks = rows // BLOCK
    weight = qkv_weight.reshape(features, 3 * columns)
    ids = lax.axis_index("band") * num_blocks + jnp.arange(num_blocks, dtype=jnp.int32)
    first = (key_start - (ids - REACH))[:, None]
    block = jnp.arange(128, dtype=jnp.int32)[None, :]
    live = (block >= first) & (block < first + key_count[:, None])
    bias = jnp.where(live, 0.0, DEAD).astype(F32)
    whole = pl.BlockSpec(memory_space=pltpu.VMEM)
    far = pl.BlockSpec(memory_space=pl.ANY)
    return pl.pallas_call(
        layer,
        out_shape=jax.ShapeDtypeStruct((HALF, features), BF16),
        in_specs=[far, whole, far, whole, far, whole],
        out_specs=whole,
        scratch_shapes=[
            pltpu.VMEM((rows, features), BF16),
            pltpu.VMEM((features, 3 * columns), BF16),
            pltpu.VMEM((features, features), BF16),
            pltpu.VMEM((6 * WIDE, 256), BF16),
            pltpu.VMEM((rows, 128), BF16),
            pltpu.VMEM((rows, 128), BF16),
            pltpu.VMEM((HALF, features), BF16),
            pltpu.VMEM((HALF, features), BF16),
            pltpu.SemaphoreType.DMA((4,)),
            pltpu.SemaphoreType.DMA((3,)),
            pltpu.SemaphoreType.DMA((2,)),
            pltpu.SemaphoreType.DMA((2,)),
            pltpu.SemaphoreType.DMA((7,)),
            pltpu.SemaphoreType.DMA((8,)),
            pltpu.SemaphoreType.DMA,
        ],
        compiler_params=pltpu.CompilerParams(
            vmem_limit_bytes=56 << 20, collective_id=0, has_side_effects=True
        ),
        name="layer",
    )(tokens, ln_gain.reshape(1, features), weight, qk_gain.reshape(2, columns), out_weight, bias)


def solution(mesh):
    placed = (
        P(("member", "band"), None),
        P(),
        P(None, None, "head"),
        P(None, "head", None),
        P(),
        P("band"),
        P("band"),
    )
    return jax.shard_map(
        on_device,
        mesh=mesh,
        in_specs=placed,
        out_specs=P(("member", "band", "head"), None),
        check_vma=False,
    )
```

```python
import jax
import jax.numpy as jnp
from jax import lax
from jax.experimental import pallas as pl
from jax.experimental.pallas import tpu as pltpu
from jax.sharding import PartitionSpec as P

BLOCK = 128
REACH = 7
WIDE = REACH * BLOCK
SPAN = (2 * REACH + 1) * BLOCK
HALF = WIDE // 2
STEP = 448
CHUNK = 256
LOG2E = 1.4426950408889634
DEAD = -30000.0
F32 = jnp.float32
BF16 = jnp.bfloat16
MESH = pl.DeviceIdType.MESH


def pair_ones():
    row = lax.broadcasted_iota(jnp.int32, (256, 128), 0)
    col = lax.broadcasted_iota(jnp.int32, (256, 128), 1)
    return (((row // 64) % 2) == (col // 64)).astype(BF16)


def layer_normed(values, gain):
    center = jnp.mean(values, axis=-1, keepdims=True)
    shifted = values - center
    spread = jnp.mean(jnp.square(shifted), axis=-1, keepdims=True)
    return (shifted * lax.rsqrt(spread + 1e-05) * gain).astype(BF16)


def head_normed(raw, gain, ones):
    square = raw * raw
    high = square.astype(BF16)
    low = (square - high.astype(F32)).astype(BF16)
    total = jnp.dot(jnp.concatenate([high, low], 1), ones, preferred_element_type=F32)
    return (raw * lax.rsqrt(total * (1.0 / 64.0) + 1e-06) * gain).astype(BF16)


def rows_at(first, count):
    return pl.ds(pl.multiple_of(first, 64), count)


def attend_block(q, first_key, key_count, kv, first, lane):
    zero = jnp.zeros_like(q)
    live = (lane >= first_key) & (lane < first_key + key_count)
    bias = jnp.where(live, 0.0, DEAD).astype(BF16)
    both = jnp.concatenate(
        [
            jnp.concatenate([jnp.where(lane < 64, q, zero), bias], 1),
            jnp.concatenate([jnp.where(lane < 64, zero, q), bias], 1),
        ],
        0,
    )
    acc = None
    for j in range(0, SPAN, CHUNK):
        count = min(CHUNK, SPAN - j)
        marks = [(lane == (j // BLOCK + m)).astype(BF16) for m in range(count // BLOCK)]
        keys = jnp.concatenate([kv[rows_at(first + j, count), :128], jnp.concatenate(marks, 0)], 1)
        values = jnp.concatenate([kv[rows_at(first + j, count), 128:], jnp.ones((count, 128), BF16)], 1)
        scores = lax.dot_general(both, keys, (((1,), (1,)), ((), ())), preferred_element_type=F32)
        part = jnp.dot(jnp.exp2(scores).astype(BF16), values, preferred_element_type=F32)
        acc = part if acc is None else acc + part
    mixed = acc[:, :128] * (1.0 / acc[:, 128:])
    return jnp.where(lane < 64, mixed[:BLOCK], mixed[BLOCK:]).astype(BF16)


def layer(
    tok, ln, w_hbm, gain, ow_hbm, key_start, key_count, out,
    xv, w, wf, g, gf, ow, kv, qs, att, rcv, res,
    in_sem, w_sem, halo_send, halo_recv, give_send, give_recv, keep_sem, z_send, z_recv, xy_send, xy_recv,
):
    band = lax.axis_index("band")
    head = lax.axis_index("head")
    member = lax.axis_index("member")
    bands = 16
    line = band // 4
    x = band % 4
    t = head // 2
    c = head % 2
    t_op = (t + 2) % 4
    t_a = 1 + t % 2
    t_b = 3 * ((t + 1) % 2)
    far = t_op * 2 + c

    order = (3, 0, 1, 2)
    loads = {}
    for ch in order:
        loads[ch] = pltpu.make_async_copy(
            tok.at[pl.ds(ch * WIDE, WIDE), :], xv.at[pl.ds(ch * WIDE, WIDE), :], in_sem.at[ch]
        )
    loads[3].start()
    load_w = [
        pltpu.make_async_copy(w_hbm.at[p], w.at[:, pl.ds(p * 128, 128)], w_sem.at[p]) for p in range(3)
    ]
    for copy in load_w:
        copy.start()
    for ch in order[1:]:
        loads[ch].start()
    load_ow = pltpu.make_async_copy(ow_hbm, ow, w_sem.at[3])
    load_ow.start()
    load_res = pltpu.make_async_copy(tok.at[rows_at(t * WIDE + c * HALF, HALF), :], res, w_sem.at[4])
    load_res.start()

    barrier = pltpu.get_barrier_semaphore()
    for d in range(1, 8):
        pl.semaphore_signal(barrier, inc=1, device_id={"head": (head + d) % 8}, device_id_type=MESH)
    for d in range(1, 4):
        pl.semaphore_signal(barrier, inc=1, device_id={"band": line * 4 + (x + d) % 4}, device_id_type=MESH)
        pl.semaphore_signal(barrier, inc=1, device_id={"member": (member + d) % 4}, device_id_type=MESH)

    @pl.when(x == 3)
    def _():
        pl.semaphore_signal(barrier, inc=1, device_id={"band": (band + 1) % bands}, device_id_type=MESH)

    @pl.when(x == 0)
    def _():
        pl.semaphore_signal(barrier, inc=1, device_id={"band": (band + bands - 1) % bands}, device_id_type=MESH)

    @pl.when(band == 0)
    def _():
        kv[pl.ds(0, WIDE), :] = jnp.zeros((WIDE, 256), BF16)

    @pl.when(band == bands - 1)
    def _():
        kv[pl.ds(5 * WIDE, WIDE), :] = jnp.zeros((WIDE, 256), BF16)

    @pl.when((band == 0) & (t == 0))
    def _():
        kv[pl.ds(6 * WIDE, WIDE), :] = jnp.zeros((WIDE, 256), BF16)

    @pl.when((band == bands - 1) & (t == 3))
    def _():
        kv[pl.ds(8 * WIDE, WIDE), :] = jnp.zeros((WIDE, 256), BF16)

    ones = pair_ones()
    for kind in range(2):
        g[kind : kind + 1, :] = jnp.concatenate([gain[kind, 0:1, :], gain[kind, 1:2, :]], 1)
    g[2:8, :] = jnp.zeros((6, 128), F32)

    def put_kv(raw, gains, first):
        kv[rows_at(first, STEP), :128] = head_normed(raw[:, :128], gains[1:2, :], ones)
        kv[rows_at(first, STEP), 128:] = raw[:, 128:].astype(BF16)

    def put_q(raw, gains, first):
        qs[rows_at(first, STEP), :] = head_normed(raw, gains[0:1, :] * (LOG2E / 8.0), ones)

    def project(ch):
        def step(s, carry):
            first = ch * WIDE + s * STEP
            normed = layer_normed(xv[rows_at(first, STEP), :].astype(F32), ln[...])
            xv[rows_at(first, STEP), :] = normed
            raw = jnp.dot(normed, w[...], preferred_element_type=F32)
            put_q(raw[:, :128], g, first)
            put_kv(raw[:, 128:], g, WIDE + first)
            return carry

        lax.fori_loop(0, WIDE // STEP, step, 0)

    def project_far(ch, target):
        def step(s, carry):
            normed = xv[rows_at(ch * WIDE + s * STEP, STEP), :]
            raw = jnp.dot(normed, wf[:, 128:], preferred_element_type=F32)
            put_kv(raw, gf, target + s * STEP)
            return carry

        lax.fori_loop(0, WIDE // STEP, step, 0)

    def halo(side):
        return pltpu.make_async_remote_copy(
            src_ref=kv.at[pl.ds((4 - 3 * side) * WIDE, WIDE), :],
            dst_ref=kv.at[pl.ds(5 * side * WIDE, WIDE), :],
            send_sem=halo_send.at[side],
            recv_sem=halo_recv.at[side],
            device_id={"band": band + 1 - 2 * side},
            device_id_type=MESH,
        )

    def far_halo(side):
        return pltpu.make_async_remote_copy(
            src_ref=kv.at[pl.ds(9 * WIDE, WIDE), :],
            dst_ref=kv.at[pl.ds((6 + 2 * side) * WIDE, WIDE), :],
            send_sem=halo_send.at[2],
            recv_sem=halo_recv.at[2],
            device_id={"band": band + 1 - 2 * side},
            device_id_type=MESH,
        )

    piece = rows_at(64 * (4 * member + x), 64)
    quarter = rows_at(256 * member, 256)

    def send_z(which):
        return pltpu.make_async_remote_copy(
            src_ref=(w.at[piece, :], g)[which],
            dst_ref=(wf.at[piece, :], gf)[which],
            send_sem=z_send.at[which],
            recv_sem=z_recv.at[which],
            device_id={"head": far},
            device_id_type=MESH,
        )

    def send_x(d):
        return pltpu.make_async_remote_copy(
            src_ref=wf.at[piece, :],
            dst_ref=wf.at[piece, :],
            send_sem=xy_send.at[d - 1],
            recv_sem=xy_recv.at[d - 1],
            device_id={"band": line * 4 + (x + d) % 4},
            device_id_type=MESH,
        )

    def recv_x(d):
        came = rows_at(64 * (4 * member + (x + 4 - d) % 4), 64)
        return pltpu.make_async_remote_copy(
            src_ref=wf.at[came, :],
            dst_ref=wf.at[came, :],
            send_sem=xy_send.at[d - 1],
            recv_sem=xy_recv.at[d - 1],
            device_id={"band": line * 4 + (x + 4 - d) % 4},
            device_id_type=MESH,
        )

    def send_y(d):
        return pltpu.make_async_remote_copy(
            src_ref=wf.at[quarter, :],
            dst_ref=wf.at[quarter, :],
            send_sem=xy_send.at[d + 2],
            recv_sem=xy_recv.at[d + 2],
            device_id={"member": (member + d) % 4},
            device_id_type=MESH,
        )

    def recv_y(d):
        came = rows_at(256 * ((member + 4 - d) % 4), 256)
        return pltpu.make_async_remote_copy(
            src_ref=wf.at[came, :],
            dst_ref=wf.at[came, :],
            send_sem=xy_send.at[d + 2],
            recv_sem=xy_recv.at[d + 2],
            device_id={"member": (member + 4 - d) % 4},
            device_id_type=MESH,
        )

    loads[3].wait()
    for copy in load_w:
        copy.wait()
    project(3)
    pl.semaphore_wait(barrier, 13 + (x + 1) // 4 + (4 - x) // 4)
    send_z(0).start()
    send_z(1).start()

    @pl.when(band < bands - 1)
    def _():
        halo(0).start()

    loads[0].wait()
    project(0)

    @pl.when(band > 0)
    def _():
        halo(1).start()

    loads[1].wait()
    project(1)
    send_z(0).wait_recv()
    for d in (1, 3, 2):
        send_x(d).start()
    loads[2].wait()
    project(2)

    lane = lax.broadcasted_iota(jnp.int32, (BLOCK, 128), 1)

    def give(unit, part, chip, core, slot, column):
        return pltpu.make_async_remote_copy(
            src_ref=att.at[rows_at(unit * WIDE + part * HALF, HALF), :],
            dst_ref=rcv.at[:, pl.ds(pl.multiple_of(column * 128, 128), 128)],
            send_sem=give_send.at[slot],
            recv_sem=give_recv.at[column],
            device_id={"head": chip * 2 + core},
            device_id_type=MESH,
        )

    def block(unit, chip, i, q_first, kv_first):
        local = chip * REACH + i
        att[rows_at(unit * WIDE + i * BLOCK, BLOCK), :] = attend_block(
            qs[rows_at(q_first + i * BLOCK, BLOCK), :],
            key_start[local] - (band * 4 * REACH + local - REACH),
            key_count[local],
            kv,
            kv_first + i * BLOCK,
            lane,
        )

    for i in range(7):
        block(0, t_a, i, t_a * WIDE, t_a * WIDE)
        if i == 1:
            for d in (1, 3, 2):
                recv_x(d).wait_recv()
            for d in (1, 3, 2):
                send_y(d).start()
        if i == 3:
            give(0, 0, t_a, 0, 0, head).start()
    give(0, 1, t_a, 1, 1, head).start()

    @pl.when(band > 0)
    def _():
        halo(0).wait_recv()

    @pl.when(band < bands - 1)
    def _():
        halo(1).wait_recv()

    for i in range(7):
        block(1, t_b, i, t_b * WIDE, t_b * WIDE)
        if i == 3:
            give(1, 0, t_b, 0, 2, head).start()
    give(1, 1, t_b, 1, 3, head).start()

    for d in (1, 3, 2):
        recv_y(d).wait_recv()
    send_z(1).wait_recv()
    inner = ((t + 1) // 2) % 2
    edge = 2 * (t // 2)
    project_far(t_b, (9 - inner * (3 - edge)) * WIDE)

    @pl.when((t == 0) & (band < bands - 1))
    def _():
        far_halo(0).start()

    @pl.when((t == 3) & (band > 0))
    def _():
        far_halo(1).start()

    project_far(t_a, (8 - edge) * WIDE)
    project_far(t, 7 * WIDE)

    def far_queries(s, carry):
        raw = jnp.dot(xv[rows_at(t * WIDE + s * STEP, STEP), :], wf[:, :128], preferred_element_type=F32)
        put_q(raw, gf, 4 * WIDE + s * STEP)
        return carry

    lax.fori_loop(0, WIDE // STEP, far_queries, 0)

    def keep(unit, column, sem):
        return pltpu.make_async_copy(
            att.at[rows_at(unit * WIDE + c * HALF, HALF), :],
            rcv.at[:, pl.ds(pl.multiple_of(column * 128, 128), 128)],
            keep_sem.at[sem],
        )

    for k in range(7):
        block(2, t, (k + 3 * (1 - c)) % 7, t * WIDE, t * WIDE)
        if k == 3:
            give(2, 1 - c, t, 1 - c, 4, head).start()
    keep(2, head, 0).start()

    @pl.when((t == 0) & (band > 0))
    def _():
        far_halo(0).wait_recv()

    @pl.when((t == 3) & (band < bands - 1))
    def _():
        far_halo(1).wait_recv()

    for k in range(7):
        block(3, t, (k + 3 * (1 - c)) % 7, 4 * WIDE, 6 * WIDE)
        if k == 3:
            give(3, 1 - c, t, 1 - c, 5, far).start()
    keep(3, far, 1).start()

    load_ow.wait()
    load_res.wait()
    keep(2, head, 0).wait()
    keep(3, far, 1).wait()
    up = (t + 1) % 4
    down = (t + 3) % 4
    for column in (up * 2, up * 2 + 1, down * 2, down * 2 + 1, t * 2 + 1 - c, t_op * 2 + 1 - c):
        pltpu.make_async_remote_copy(
            src_ref=att.at[pl.ds(0, HALF), :],
            dst_ref=rcv.at[:, pl.ds(pl.multiple_of(column * 128, 128), 128)],
            send_sem=give_send.at[0],
            recv_sem=give_recv.at[column],
            device_id={"head": t * 2 + 1 - c},
            device_id_type=MESH,
        ).wait_recv()
    for r in range(0, HALF, 224):
        summed = jnp.dot(rcv[pl.ds(r, 224), :], ow[...], preferred_element_type=F32)
        out[pl.ds(r, 224), :] = (res[pl.ds(r, 224), :].astype(F32) + summed).astype(BF16)
    for slot in range(4):
        chip = (t_a, t_b)[slot // 2]
        give(slot // 2, slot % 2, chip, slot % 2, slot, head).wait_send()
    give(2, 1 - c, t, 1 - c, 4, head).wait_send()
    give(3, 1 - c, t, 1 - c, 5, far).wait_send()
    send_z(0).wait_send()
    send_z(1).wait_send()
    for d in (1, 2, 3):
        send_x(d).wait_send()
        send_y(d).wait_send()

    @pl.when(band < bands - 1)
    def _():
        halo(0).wait_send()

    @pl.when(band > 0)
    def _():
        halo(1).wait_send()

    @pl.when((t == 0) & (band < bands - 1))
    def _():
        far_halo(0).wait_send()

    @pl.when((t == 3) & (band > 0))
    def _():
        far_halo(1).wait_send()


def on_device(tokens, ln_gain, qkv_weight, qk_gain, out_weight, key_start, key_count):
    rows, features = tokens.shape
    columns = qk_gain.shape[1] * qk_gain.shape[2]
    weight = jnp.transpose(qkv_weight, (1, 0, 2))
    whole = pl.BlockSpec(memory_space=pltpu.VMEM)
    scalars = pl.BlockSpec(memory_space=pltpu.SMEM)
    far = pl.BlockSpec(memory_space=pl.ANY)
    return pl.pallas_call(
        layer,
        out_shape=jax.ShapeDtypeStruct((HALF, features), BF16),
        in_specs=[far, whole, far, whole, far, scalars, scalars],
        out_specs=whole,
        scratch_shapes=[
            pltpu.VMEM((rows, features), BF16),
            pltpu.VMEM((features, 3 * columns), BF16),
            pltpu.VMEM((features, 3 * columns), BF16),
            pltpu.VMEM((8, 128), F32),
            pltpu.VMEM((8, 128), F32),
            pltpu.VMEM((features, features), BF16),
            pltpu.VMEM((10 * WIDE, 256), BF16),
            pltpu.VMEM((5 * WIDE, 128), BF16),
            pltpu.VMEM((4 * WIDE, 128), BF16),
            pltpu.VMEM((HALF, features), BF16),
            pltpu.VMEM((HALF, features), BF16),
            pltpu.SemaphoreType.DMA((4,)),
            pltpu.SemaphoreType.DMA((5,)),
            pltpu.SemaphoreType.DMA((3,)),
            pltpu.SemaphoreType.DMA((3,)),
            pltpu.SemaphoreType.DMA((6,)),
            pltpu.SemaphoreType.DMA((8,)),
            pltpu.SemaphoreType.DMA((2,)),
            pltpu.SemaphoreType.DMA((2,)),
            pltpu.SemaphoreType.DMA((2,)),
            pltpu.SemaphoreType.DMA((6,)),
            pltpu.SemaphoreType.DMA((6,)),
        ],
        compiler_params=pltpu.CompilerParams(
            vmem_limit_bytes=56 << 20, collective_id=0, has_side_effects=True
        ),
        name="layer",
    )(tokens, ln_gain.reshape(1, features), weight, qk_gain, out_weight, key_start, key_count)


def solution(mesh):
    placed = (
        P(("member", "band"), None),
        P(),
        P(None, None, "head"),
        P(None, "head", None),
        P(),
        P("band"),
        P("band"),
    )
    return jax.shard_map(
        on_device,
        mesh=mesh,
        in_specs=placed,
        out_specs=P(("member", "band", "head"), None),
        check_vma=False,
    )
```

```python
import jax
import jax.numpy as jnp
from jax import lax
from jax.experimental import pallas as pl
from jax.experimental.pallas import tpu as pltpu
from jax.sharding import PartitionSpec as P

BLOCK = 128
REACH = 7
WIDE = REACH * BLOCK
SPAN = (2 * REACH + 1) * BLOCK
HALF = WIDE // 2
STEP = 448
CHUNK = 256
LOG2E = 1.4426950408889634
DEAD = -30000.0
F32 = jnp.float32
BF16 = jnp.bfloat16
MESH = pl.DeviceIdType.MESH


def pair_ones():
    row = lax.broadcasted_iota(jnp.int32, (256, 128), 0)
    col = lax.broadcasted_iota(jnp.int32, (256, 128), 1)
    return (((row // 64) % 2) == (col // 64)).astype(BF16)


def layer_normed(values, gain):
    center = jnp.mean(values, axis=-1, keepdims=True)
    shifted = values - center
    spread = jnp.mean(jnp.square(shifted), axis=-1, keepdims=True)
    return (shifted * lax.rsqrt(spread + 1e-05) * gain).astype(BF16)


def head_normed(raw, gain, ones):
    square = raw * raw
    high = square.astype(BF16)
    low = (square - high.astype(F32)).astype(BF16)
    total = jnp.dot(jnp.concatenate([high, low], 1), ones, preferred_element_type=F32)
    return (raw * lax.rsqrt(total * (1.0 / 64.0) + 1e-06) * gain).astype(BF16)


def rows_at(first, count):
    return pl.ds(pl.multiple_of(first, 64), count)


def attend_block(q, first_key, key_count, kv, first, lane):
    zero = jnp.zeros_like(q)
    live = (lane >= first_key) & (lane < first_key + key_count)
    bias = jnp.where(live, 0.0, DEAD).astype(BF16)
    both = jnp.concatenate(
        [
            jnp.concatenate([jnp.where(lane < 64, q, zero), bias], 1),
            jnp.concatenate([jnp.where(lane < 64, zero, q), bias], 1),
        ],
        0,
    )
    acc = None
    for j in range(0, SPAN, CHUNK):
        count = min(CHUNK, SPAN - j)
        marks = [(lane == (j // BLOCK + m)).astype(BF16) for m in range(count // BLOCK)]
        keys = jnp.concatenate([kv[rows_at(first + j, count), :128], jnp.concatenate(marks, 0)], 1)
        values = jnp.concatenate([kv[rows_at(first + j, count), 128:], jnp.ones((count, 128), BF16)], 1)
        scores = lax.dot_general(both, keys, (((1,), (1,)), ((), ())), preferred_element_type=F32)
        part = jnp.dot(jnp.exp2(scores).astype(BF16), values, preferred_element_type=F32)
        acc = part if acc is None else acc + part
    mixed = acc[:, :128] * (1.0 / acc[:, 128:])
    return jnp.where(lane < 64, mixed[:BLOCK], mixed[BLOCK:]).astype(BF16)


def attend_part(q, first_key, key_count, kv, first, lane, count):
    zero = jnp.zeros_like(q)
    live = (lane >= first_key) & (lane < first_key + key_count)
    bias = jnp.where(live, 0.0, DEAD).astype(BF16)
    both = jnp.concatenate(
        [
            jnp.concatenate([jnp.where(lane < 64, q, zero), bias], 1),
            jnp.concatenate([jnp.where(lane < 64, zero, q), bias], 1),
        ],
        0,
    )
    acc = None
    for j in range(0, count * BLOCK, CHUNK):
        size = min(CHUNK, count * BLOCK - j)
        marks = [(lane == (j // BLOCK + m)).astype(BF16) for m in range(size // BLOCK)]
        keys = jnp.concatenate([kv[rows_at(first + j, size), :128], jnp.concatenate(marks, 0)], 1)
        values = jnp.concatenate([kv[rows_at(first + j, size), 128:], jnp.ones((size, 128), BF16)], 1)
        scores = lax.dot_general(both, keys, (((1,), (1,)), ((), ())), preferred_element_type=F32)
        part = jnp.dot(jnp.exp2(scores).astype(BF16), values, preferred_element_type=F32)
        acc = part if acc is None else acc + part
    return acc


def layer(
    tok, ln, w_hbm, gain, ow_hbm, key_start, key_count, out,
    xv, w, wf, g, gf, ow, kv, qs, acc, total, att, rcv, res,
    in_sem, w_sem, halo_send, halo_recv, give_send, give_recv, keep_sem, z_send, z_recv, xy_send, xy_recv,
):
    band = lax.axis_index("band")
    head = lax.axis_index("head")
    member = lax.axis_index("member")
    bands = 16
    line = band // 4
    x = band % 4
    t = head // 2
    c = head % 2
    t_op = (t + 2) % 4
    t_a = 1 + t % 2
    t_b = 3 * ((t + 1) % 2)
    far = t_op * 2 + c

    order = (3, 0, 1, 2)
    loads = {}
    for ch in order:
        loads[ch] = pltpu.make_async_copy(
            tok.at[pl.ds(ch * WIDE, WIDE), :], xv.at[pl.ds(ch * WIDE, WIDE), :], in_sem.at[ch]
        )
    loads[3].start()
    load_w = [
        pltpu.make_async_copy(w_hbm.at[p], w.at[:, pl.ds(p * 128, 128)], w_sem.at[p]) for p in range(3)
    ]
    for copy in load_w:
        copy.start()
    for ch in order[1:]:
        loads[ch].start()
    load_ow = pltpu.make_async_copy(ow_hbm, ow, w_sem.at[3])
    load_ow.start()
    load_res = pltpu.make_async_copy(tok.at[rows_at(t * WIDE + c * HALF, HALF), :], res, w_sem.at[4])
    load_res.start()

    barrier = pltpu.get_barrier_semaphore()
    for d in range(1, 8):
        pl.semaphore_signal(barrier, inc=1, device_id={"head": (head + d) % 8}, device_id_type=MESH)
    for d in range(1, 4):
        pl.semaphore_signal(barrier, inc=1, device_id={"band": line * 4 + (x + d) % 4}, device_id_type=MESH)
        pl.semaphore_signal(barrier, inc=1, device_id={"member": (member + d) % 4}, device_id_type=MESH)

    @pl.when(x == 3)
    def _():
        pl.semaphore_signal(barrier, inc=1, device_id={"band": (band + 1) % bands}, device_id_type=MESH)

    @pl.when(x == 0)
    def _():
        pl.semaphore_signal(barrier, inc=1, device_id={"band": (band + bands - 1) % bands}, device_id_type=MESH)

    @pl.when(band == 0)
    def _():
        kv[pl.ds(0, WIDE), :] = jnp.zeros((WIDE, 256), BF16)

    @pl.when(band == bands - 1)
    def _():
        kv[pl.ds(5 * WIDE, WIDE), :] = jnp.zeros((WIDE, 256), BF16)

    @pl.when((band == 0) & (t == 0))
    def _():
        kv[pl.ds(6 * WIDE, WIDE), :] = jnp.zeros((WIDE, 256), BF16)

    @pl.when((band == bands - 1) & (t == 3))
    def _():
        kv[pl.ds(8 * WIDE, WIDE), :] = jnp.zeros((WIDE, 256), BF16)

    ones = pair_ones()
    for kind in range(2):
        g[kind : kind + 1, :] = jnp.concatenate([gain[kind, 0:1, :], gain[kind, 1:2, :]], 1)
    g[2:8, :] = jnp.zeros((6, 128), F32)

    def put_kv(raw, gains, first):
        kv[rows_at(first, STEP), :128] = head_normed(raw[:, :128], gains[1:2, :], ones)
        kv[rows_at(first, STEP), 128:] = raw[:, 128:].astype(BF16)

    def put_q(raw, gains, first):
        qs[rows_at(first, STEP), :] = head_normed(raw, gains[0:1, :] * (LOG2E / 8.0), ones)

    def project(ch):
        def step(s, carry):
            first = ch * WIDE + s * STEP
            normed = layer_normed(xv[rows_at(first, STEP), :].astype(F32), ln[...])
            xv[rows_at(first, STEP), :] = normed
            raw = jnp.dot(normed, w[...], preferred_element_type=F32)
            put_q(raw[:, :128], g, first)
            put_kv(raw[:, 128:], g, WIDE + first)
            return carry

        lax.fori_loop(0, WIDE // STEP, step, 0)

    def project_far(ch, target):
        def step(s, carry):
            normed = xv[rows_at(ch * WIDE + s * STEP, STEP), :]
            raw = jnp.dot(normed, wf[:, 128:], preferred_element_type=F32)
            put_kv(raw, gf, target + s * STEP)
            return carry

        lax.fori_loop(0, WIDE // STEP, step, 0)

    def halo(side):
        return pltpu.make_async_remote_copy(
            src_ref=kv.at[pl.ds((4 - 3 * side) * WIDE, WIDE), :],
            dst_ref=kv.at[pl.ds(5 * side * WIDE, WIDE), :],
            send_sem=halo_send.at[side],
            recv_sem=halo_recv.at[side],
            device_id={"band": band + 1 - 2 * side},
            device_id_type=MESH,
        )

    def far_halo(side):
        return pltpu.make_async_remote_copy(
            src_ref=kv.at[pl.ds(9 * WIDE, WIDE), :],
            dst_ref=kv.at[pl.ds((6 + 2 * side) * WIDE, WIDE), :],
            send_sem=halo_send.at[2],
            recv_sem=halo_recv.at[2],
            device_id={"band": band + 1 - 2 * side},
            device_id_type=MESH,
        )

    piece = rows_at(64 * (4 * member + x), 64)
    quarter = rows_at(256 * member, 256)

    def send_z(which):
        return pltpu.make_async_remote_copy(
            src_ref=(w.at[piece, :], g)[which],
            dst_ref=(wf.at[piece, :], gf)[which],
            send_sem=z_send.at[which],
            recv_sem=z_recv.at[which],
            device_id={"head": far},
            device_id_type=MESH,
        )

    def send_x(d):
        return pltpu.make_async_remote_copy(
            src_ref=wf.at[piece, :],
            dst_ref=wf.at[piece, :],
            send_sem=xy_send.at[d - 1],
            recv_sem=xy_recv.at[d - 1],
            device_id={"band": line * 4 + (x + d) % 4},
            device_id_type=MESH,
        )

    def recv_x(d):
        came = rows_at(64 * (4 * member + (x + 4 - d) % 4), 64)
        return pltpu.make_async_remote_copy(
            src_ref=wf.at[came, :],
            dst_ref=wf.at[came, :],
            send_sem=xy_send.at[d - 1],
            recv_sem=xy_recv.at[d - 1],
            device_id={"band": line * 4 + (x + 4 - d) % 4},
            device_id_type=MESH,
        )

    def send_y(d):
        return pltpu.make_async_remote_copy(
            src_ref=wf.at[quarter, :],
            dst_ref=wf.at[quarter, :],
            send_sem=xy_send.at[d + 2],
            recv_sem=xy_recv.at[d + 2],
            device_id={"member": (member + d) % 4},
            device_id_type=MESH,
        )

    def recv_y(d):
        came = rows_at(256 * ((member + 4 - d) % 4), 256)
        return pltpu.make_async_remote_copy(
            src_ref=wf.at[came, :],
            dst_ref=wf.at[came, :],
            send_sem=xy_send.at[d + 2],
            recv_sem=xy_recv.at[d + 2],
            device_id={"member": (member + 4 - d) % 4},
            device_id_type=MESH,
        )

    loads[3].wait()
    for copy in load_w:
        copy.wait()
    project(3)
    pl.semaphore_wait(barrier, 13 + (x + 1) // 4 + (4 - x) // 4)
    send_z(0).start()
    send_z(1).start()

    @pl.when(band < bands - 1)
    def _():
        halo(0).start()

    loads[0].wait()
    project(0)

    @pl.when(band > 0)
    def _():
        halo(1).start()

    loads[1].wait()
    project(1)
    send_z(0).wait_recv()
    for d in (1, 3, 2):
        send_x(d).start()
    loads[2].wait()
    project(2)

    lane = lax.broadcasted_iota(jnp.int32, (BLOCK, 128), 1)

    def give(unit, part, chip, core, slot, column):
        return pltpu.make_async_remote_copy(
            src_ref=att.at[rows_at(unit * WIDE + part * HALF, HALF), :],
            dst_ref=rcv.at[:, pl.ds(pl.multiple_of(column * 128, 128), 128)],
            send_sem=give_send.at[slot],
            recv_sem=give_recv.at[column],
            device_id={"head": chip * 2 + core},
            device_id_type=MESH,
        )

    def block(unit, chip, i, q_first, kv_first):
        local = chip * REACH + i
        att[rows_at(unit * WIDE + i * BLOCK, BLOCK), :] = attend_block(
            qs[rows_at(q_first + i * BLOCK, BLOCK), :],
            key_start[local] - (band * 4 * REACH + local - REACH),
            key_count[local],
            kv,
            kv_first + i * BLOCK,
            lane,
        )

    for i in range(7):
        block(0, t_a, i, t_a * WIDE, t_a * WIDE)
        if i == 1:
            for d in (1, 3, 2):
                recv_x(d).wait_recv()
            for d in (1, 3, 2):
                send_y(d).start()
        if i == 3:
            give(0, 0, t_a, 0, 0, head).start()
    give(0, 1, t_a, 1, 1, head).start()

    @pl.when(band > 0)
    def _():
        halo(0).wait_recv()

    @pl.when(band < bands - 1)
    def _():
        halo(1).wait_recv()

    for i in range(7):
        block(1, t_b, i, t_b * WIDE, t_b * WIDE)
        if i == 3:
            give(1, 0, t_b, 0, 2, head).start()
    give(1, 1, t_b, 1, 3, head).start()

    for d in (1, 3, 2):
        recv_y(d).wait_recv()
    send_z(1).wait_recv()
    inner = ((t + 1) // 2) % 2
    edge = 2 * (t // 2)
    project_far(t_b, (9 - inner * (3 - edge)) * WIDE)

    @pl.when((t == 0) & (band < bands - 1))
    def _():
        far_halo(0).start()

    @pl.when((t == 3) & (band > 0))
    def _():
        far_halo(1).start()

    project_far(t_a, (8 - edge) * WIDE)
    project_far(t, 7 * WIDE)

    def far_queries(s, carry):
        raw = jnp.dot(xv[rows_at(t * WIDE + s * STEP, STEP), :], wf[:, :128], preferred_element_type=F32)
        put_q(raw, gf, 4 * WIDE + s * STEP)
        return carry

    lax.fori_loop(0, WIDE // STEP, far_queries, 0)

    def keep(unit, column, sem):
        return pltpu.make_async_copy(
            att.at[rows_at(unit * WIDE + c * HALF, HALF), :],
            rcv.at[:, pl.ds(pl.multiple_of(column * 128, 128), 128)],
            keep_sem.at[sem],
        )

    for k in range(7):
        block(2, t, (k + 3 * (1 - c)) % 7, t * WIDE, t * WIDE)
        if k == 3:
            give(2, 1 - c, t, 1 - c, 4, head).start()
    keep(2, head, 0).start()

    hi = t // 2

    def part(k, count, base, skip):
        i = k + hi * (6 - 2 * k)
        local = t * REACH + i
        return i, attend_part(
            qs[rows_at(4 * WIDE + i * BLOCK, BLOCK), :],
            key_start[local] - (band * 4 * REACH + local - REACH) - skip,
            key_count[local],
            kv,
            6 * WIDE + base * BLOCK,
            lane,
            count,
        )

    for k in range(7):
        _, sums = part(k, 8 + k, 7 * (1 - hi) + hi * (6 - k), (1 - hi) * (7 - k))
        acc[pl.ds(k * 256, 256), :] = sums

    load_ow.wait()
    load_res.wait()
    keep(2, head, 0).wait()

    def arrive(column):
        pltpu.make_async_remote_copy(
            src_ref=att.at[pl.ds(0, HALF), :],
            dst_ref=rcv.at[:, pl.ds(pl.multiple_of(column * 128, 128), 128)],
            send_sem=give_send.at[0],
            recv_sem=give_recv.at[column],
            device_id={"head": t * 2 + 1 - c},
            device_id_type=MESH,
        ).wait_recv()

    def out_part(chip, r):
        columns = pl.ds(pl.multiple_of(chip * 256, 256), 256)
        return jnp.dot(rcv[pl.ds(r, 224), columns], ow[columns, :], preferred_element_type=F32)

    def edge_part(k):
        i, sums = part(k, 7 - k, (1 - hi) * k + 14 * hi, hi * (8 + k))
        sums = sums + acc[pl.ds(k * 256, 256), :]
        mixed = sums[:, :128] * (1.0 / sums[:, 128:])
        att[rows_at(3 * WIDE + i * BLOCK, BLOCK), :] = jnp.where(lane < 64, mixed[:BLOCK], mixed[BLOCK:]).astype(BF16)

    def edges(ks):
        for n, k in enumerate(ks):
            edge_part(k)
            if n == 3:
                give(3, 1 - c, t, 1 - c, 5, far).start()

    def first_parts():
        up = (t + 1) % 4
        down = (t + 3) % 4
        for column in (t * 2 + 1 - c, up * 2, up * 2 + 1, down * 2, down * 2 + 1):
            arrive(column)
        for r in range(0, HALF, 224):
            base = res[pl.ds(r, 224), :].astype(F32)
            total[pl.ds(r, 224), :] = base + (out_part(t, r) + out_part(up, r) + out_part(down, r))

    outer = (t == 0) | (t == 3)

    @pl.when(outer)
    def _():
        first_parts()

    @pl.when((t == 0) & (band > 0))
    def _():
        far_halo(0).wait_recv()

    @pl.when((t == 3) & (band < bands - 1))
    def _():
        far_halo(1).wait_recv()

    @pl.when((c + hi) % 2 == 1)
    def _():
        edges((0, 1, 2, 3, 4, 5, 6))

    @pl.when((c + hi) % 2 == 0)
    def _():
        edges((6, 5, 4, 3, 2, 1, 0))

    keep(3, far, 1).start()

    @pl.when((t == 1) | (t == 2))
    def _():
        first_parts()

    keep(3, far, 1).wait()
    arrive(t_op * 2 + 1 - c)
    for r in range(0, HALF, 224):
        out[pl.ds(r, 224), :] = (total[pl.ds(r, 224), :] + out_part(t_op, r)).astype(BF16)
    for slot in range(4):
        chip = (t_a, t_b)[slot // 2]
        give(slot // 2, slot % 2, chip, slot % 2, slot, head).wait_send()
    give(2, 1 - c, t, 1 - c, 4, head).wait_send()
    give(3, 1 - c, t, 1 - c, 5, far).wait_send()
    send_z(0).wait_send()
    send_z(1).wait_send()
    for d in (1, 2, 3):
        send_x(d).wait_send()
        send_y(d).wait_send()

    @pl.when(band < bands - 1)
    def _():
        halo(0).wait_send()

    @pl.when(band > 0)
    def _():
        halo(1).wait_send()

    @pl.when((t == 0) & (band < bands - 1))
    def _():
        far_halo(0).wait_send()

    @pl.when((t == 3) & (band > 0))
    def _():
        far_halo(1).wait_send()


def on_device(tokens, ln_gain, qkv_weight, qk_gain, out_weight, key_start, key_count):
    rows, features = tokens.shape
    columns = qk_gain.shape[1] * qk_gain.shape[2]
    weight = jnp.transpose(qkv_weight, (1, 0, 2))
    whole = pl.BlockSpec(memory_space=pltpu.VMEM)
    scalars = pl.BlockSpec(memory_space=pltpu.SMEM)
    far = pl.BlockSpec(memory_space=pl.ANY)
    return pl.pallas_call(
        layer,
        out_shape=jax.ShapeDtypeStruct((HALF, features), BF16),
        in_specs=[far, whole, far, whole, far, scalars, scalars],
        out_specs=whole,
        scratch_shapes=[
            pltpu.VMEM((rows, features), BF16),
            pltpu.VMEM((features, 3 * columns), BF16),
            pltpu.VMEM((features, 3 * columns), BF16),
            pltpu.VMEM((8, 128), F32),
            pltpu.VMEM((8, 128), F32),
            pltpu.VMEM((features, features), BF16),
            pltpu.VMEM((10 * WIDE, 256), BF16),
            pltpu.VMEM((5 * WIDE, 128), BF16),
            pltpu.VMEM((REACH * 256, 256), F32),
            pltpu.VMEM((HALF, features), F32),
            pltpu.VMEM((4 * WIDE, 128), BF16),
            pltpu.VMEM((HALF, features), BF16),
            pltpu.VMEM((HALF, features), BF16),
            pltpu.SemaphoreType.DMA((4,)),
            pltpu.SemaphoreType.DMA((5,)),
            pltpu.SemaphoreType.DMA((3,)),
            pltpu.SemaphoreType.DMA((3,)),
            pltpu.SemaphoreType.DMA((6,)),
            pltpu.SemaphoreType.DMA((8,)),
            pltpu.SemaphoreType.DMA((2,)),
            pltpu.SemaphoreType.DMA((2,)),
            pltpu.SemaphoreType.DMA((2,)),
            pltpu.SemaphoreType.DMA((6,)),
            pltpu.SemaphoreType.DMA((6,)),
        ],
        compiler_params=pltpu.CompilerParams(
            vmem_limit_bytes=56 << 20, collective_id=0, has_side_effects=True
        ),
        name="layer",
    )(tokens, ln_gain.reshape(1, features), weight, qk_gain, out_weight, key_start, key_count)


def solution(mesh):
    placed = (
        P(("member", "band"), None),
        P(),
        P(None, None, "head"),
        P(None, "head", None),
        P(),
        P("band"),
        P("band"),
    )
    return jax.shard_map(
        on_device,
        mesh=mesh,
        in_specs=placed,
        out_specs=P(("member", "band", "head"), None),
        check_vma=False,
    )
```

```python
import jax
import jax.numpy as jnp
from jax import lax
from jax.experimental import pallas as pl
from jax.experimental.pallas import tpu as pltpu
from jax.sharding import PartitionSpec as P

BLOCK = 128
REACH = 7
WIDE = REACH * BLOCK
SPAN = (2 * REACH + 1) * BLOCK
HALF = WIDE // 2
STEP = 448
CHUNK = 256
LOG2E = 1.4426950408889634
DEAD = -30000.0
F32 = jnp.float32
BF16 = jnp.bfloat16
MESH = pl.DeviceIdType.MESH


def pair_ones():
    row = lax.broadcasted_iota(jnp.int32, (256, 128), 0)
    col = lax.broadcasted_iota(jnp.int32, (256, 128), 1)
    return (((row // 64) % 2) == (col // 64)).astype(BF16)


def layer_normed(values, gain):
    center = jnp.mean(values, axis=-1, keepdims=True)
    shifted = values - center
    spread = jnp.mean(jnp.square(shifted), axis=-1, keepdims=True)
    return (shifted * lax.rsqrt(spread + 1e-05) * gain).astype(BF16)


def head_normed(raw, gain, ones):
    square = raw * raw
    high = square.astype(BF16)
    low = (square - high.astype(F32)).astype(BF16)
    total = jnp.dot(jnp.concatenate([high, low], 1), ones, preferred_element_type=F32)
    return (raw * lax.rsqrt(total * (1.0 / 64.0) + 1e-06) * gain).astype(BF16)


def rows_at(first, count):
    return pl.ds(pl.multiple_of(first, 64), count)


def attend_block(q, first_key, key_count, kv, first, lane):
    zero = jnp.zeros_like(q)
    live = (lane >= first_key) & (lane < first_key + key_count)
    bias = jnp.where(live, 0.0, DEAD).astype(BF16)
    both = jnp.concatenate(
        [
            jnp.concatenate([jnp.where(lane < 64, q, zero), bias], 1),
            jnp.concatenate([jnp.where(lane < 64, zero, q), bias], 1),
        ],
        0,
    )
    acc = None
    for j in range(0, SPAN, CHUNK):
        count = min(CHUNK, SPAN - j)
        marks = [(lane == (j // BLOCK + m)).astype(BF16) for m in range(count // BLOCK)]
        keys = jnp.concatenate([kv[rows_at(first + j, count), :128], jnp.concatenate(marks, 0)], 1)
        values = jnp.concatenate([kv[rows_at(first + j, count), 128:], jnp.ones((count, 128), BF16)], 1)
        scores = lax.dot_general(both, keys, (((1,), (1,)), ((), ())), preferred_element_type=F32)
        part = jnp.dot(jnp.exp2(scores).astype(BF16), values, preferred_element_type=F32)
        acc = part if acc is None else acc + part
    mixed = acc[:, :128] * (1.0 / acc[:, 128:])
    return jnp.where(lane < 64, mixed[:BLOCK], mixed[BLOCK:]).astype(BF16)


def attend_part(q, first_key, key_count, kv, first, lane, count):
    zero = jnp.zeros_like(q)
    live = (lane >= first_key) & (lane < first_key + key_count)
    bias = jnp.where(live, 0.0, DEAD).astype(BF16)
    both = jnp.concatenate(
        [
            jnp.concatenate([jnp.where(lane < 64, q, zero), bias], 1),
            jnp.concatenate([jnp.where(lane < 64, zero, q), bias], 1),
        ],
        0,
    )
    acc = None
    for j in range(0, count * BLOCK, CHUNK):
        size = min(CHUNK, count * BLOCK - j)
        marks = [(lane == (j // BLOCK + m)).astype(BF16) for m in range(size // BLOCK)]
        keys = jnp.concatenate([kv[rows_at(first + j, size), :128], jnp.concatenate(marks, 0)], 1)
        values = jnp.concatenate([kv[rows_at(first + j, size), 128:], jnp.ones((size, 128), BF16)], 1)
        scores = lax.dot_general(both, keys, (((1,), (1,)), ((), ())), preferred_element_type=F32)
        part = jnp.dot(jnp.exp2(scores).astype(BF16), values, preferred_element_type=F32)
        acc = part if acc is None else acc + part
    return acc


def layer(
    tok, ln, w_hbm, gain, ow_hbm, key_start, key_count, out,
    xv, w, wf, g, gf, ow, kv, qs, acc, total, att, rcv, res,
    in_sem, w_sem, halo_send, halo_recv, give_send, give_recv, keep_sem, z_send, z_recv, xy_send, xy_recv,
):
    band = lax.axis_index("band")
    head = lax.axis_index("head")
    member = lax.axis_index("member")
    bands = 16
    line = band // 4
    x = band % 4
    t = head // 2
    c = head % 2
    t_op = (t + 2) % 4
    t_a = 1 + t % 2
    t_b = 3 * ((t + 1) % 2)
    far = t_op * 2 + c

    order = (3, 0, 1, 2)
    loads = {}
    for ch in order:
        loads[ch] = pltpu.make_async_copy(
            tok.at[pl.ds(ch * WIDE, WIDE), :], xv.at[pl.ds(ch * WIDE, WIDE), :], in_sem.at[ch]
        )
    loads[3].start()
    load_w = [
        pltpu.make_async_copy(w_hbm.at[p], w.at[:, pl.ds(p * 128, 128)], w_sem.at[p]) for p in range(3)
    ]
    for copy in load_w:
        copy.start()
    for ch in order[1:]:
        loads[ch].start()
    load_ow = pltpu.make_async_copy(ow_hbm, ow, w_sem.at[3])
    load_ow.start()
    load_res = pltpu.make_async_copy(tok.at[rows_at(t * WIDE + c * HALF, HALF), :], res, w_sem.at[4])
    load_res.start()

    barrier = pltpu.get_barrier_semaphore()
    for d in range(1, 8):
        pl.semaphore_signal(barrier, inc=1, device_id={"head": (head + d) % 8}, device_id_type=MESH)
    for d in range(1, 4):
        pl.semaphore_signal(barrier, inc=1, device_id={"band": line * 4 + (x + d) % 4}, device_id_type=MESH)
        pl.semaphore_signal(barrier, inc=1, device_id={"member": (member + d) % 4}, device_id_type=MESH)

    @pl.when(x == 3)
    def _():
        pl.semaphore_signal(barrier, inc=1, device_id={"band": (band + 1) % bands}, device_id_type=MESH)

    @pl.when(x == 0)
    def _():
        pl.semaphore_signal(barrier, inc=1, device_id={"band": (band + bands - 1) % bands}, device_id_type=MESH)

    @pl.when(band == 0)
    def _():
        kv[pl.ds(0, WIDE), :] = jnp.zeros((WIDE, 256), BF16)

    @pl.when(band == bands - 1)
    def _():
        kv[pl.ds(5 * WIDE, WIDE), :] = jnp.zeros((WIDE, 256), BF16)

    @pl.when((band == 0) & (t == 0))
    def _():
        kv[pl.ds(6 * WIDE, WIDE), :] = jnp.zeros((WIDE, 256), BF16)

    @pl.when((band == bands - 1) & (t == 3))
    def _():
        kv[pl.ds(8 * WIDE, WIDE), :] = jnp.zeros((WIDE, 256), BF16)

    ones = pair_ones()
    for kind in range(2):
        g[kind : kind + 1, :] = jnp.concatenate([gain[kind, 0:1, :], gain[kind, 1:2, :]], 1)
    g[2:8, :] = jnp.zeros((6, 128), F32)

    def put_kv(raw, gains, first):
        kv[rows_at(first, STEP), :128] = head_normed(raw[:, :128], gains[1:2, :], ones)
        kv[rows_at(first, STEP), 128:] = raw[:, 128:].astype(BF16)

    def put_q(raw, gains, first):
        qs[rows_at(first, STEP), :] = head_normed(raw, gains[0:1, :] * (LOG2E / 8.0), ones)

    def project(ch):
        def step(s, carry):
            first = ch * WIDE + s * STEP
            normed = layer_normed(xv[rows_at(first, STEP), :].astype(F32), ln[...])
            xv[rows_at(first, STEP), :] = normed
            raw = jnp.dot(normed, w[...], preferred_element_type=F32)
            put_q(raw[:, :128], g, first)
            put_kv(raw[:, 128:], g, WIDE + first)
            return carry

        lax.fori_loop(0, WIDE // STEP, step, 0)

    def project_far(ch, target):
        def step(s, carry):
            normed = xv[rows_at(ch * WIDE + s * STEP, STEP), :]
            raw = jnp.dot(normed, wf[:, 128:], preferred_element_type=F32)
            put_kv(raw, gf, target + s * STEP)
            return carry

        lax.fori_loop(0, WIDE // STEP, step, 0)

    def halo(side):
        return pltpu.make_async_remote_copy(
            src_ref=kv.at[pl.ds((4 - 3 * side) * WIDE, WIDE), :],
            dst_ref=kv.at[pl.ds(5 * side * WIDE, WIDE), :],
            send_sem=halo_send.at[side],
            recv_sem=halo_recv.at[side],
            device_id={"band": band + 1 - 2 * side},
            device_id_type=MESH,
        )

    def far_halo(side):
        return pltpu.make_async_remote_copy(
            src_ref=kv.at[pl.ds(9 * WIDE, WIDE), :],
            dst_ref=kv.at[pl.ds((6 + 2 * side) * WIDE, WIDE), :],
            send_sem=halo_send.at[2],
            recv_sem=halo_recv.at[2],
            device_id={"band": band + 1 - 2 * side},
            device_id_type=MESH,
        )

    piece = rows_at(64 * (4 * member + x), 64)
    quarter = rows_at(256 * member, 256)

    def send_z(which):
        return pltpu.make_async_remote_copy(
            src_ref=(w.at[piece, :], g)[which],
            dst_ref=(wf.at[piece, :], gf)[which],
            send_sem=z_send.at[which],
            recv_sem=z_recv.at[which],
            device_id={"head": far},
            device_id_type=MESH,
        )

    def send_x(d):
        return pltpu.make_async_remote_copy(
            src_ref=wf.at[piece, :],
            dst_ref=wf.at[piece, :],
            send_sem=xy_send.at[d - 1],
            recv_sem=xy_recv.at[d - 1],
            device_id={"band": line * 4 + (x + d) % 4},
            device_id_type=MESH,
        )

    def recv_x(d):
        came = rows_at(64 * (4 * member + (x + 4 - d) % 4), 64)
        return pltpu.make_async_remote_copy(
            src_ref=wf.at[came, :],
            dst_ref=wf.at[came, :],
            send_sem=xy_send.at[d - 1],
            recv_sem=xy_recv.at[d - 1],
            device_id={"band": line * 4 + (x + 4 - d) % 4},
            device_id_type=MESH,
        )

    def send_y(d):
        return pltpu.make_async_remote_copy(
            src_ref=wf.at[quarter, :],
            dst_ref=wf.at[quarter, :],
            send_sem=xy_send.at[d + 2],
            recv_sem=xy_recv.at[d + 2],
            device_id={"member": (member + d) % 4},
            device_id_type=MESH,
        )

    def recv_y(d):
        came = rows_at(256 * ((member + 4 - d) % 4), 256)
        return pltpu.make_async_remote_copy(
            src_ref=wf.at[came, :],
            dst_ref=wf.at[came, :],
            send_sem=xy_send.at[d + 2],
            recv_sem=xy_recv.at[d + 2],
            device_id={"member": (member + 4 - d) % 4},
            device_id_type=MESH,
        )

    loads[3].wait()
    for copy in load_w:
        copy.wait()
    project(3)
    pl.semaphore_wait(barrier, 13 + (x + 1) // 4 + (4 - x) // 4)
    send_z(0).start()
    send_z(1).start()

    @pl.when((band < bands - 1) & (t != 2))
    def _():
        halo(0).start()

    loads[0].wait()
    project(0)

    @pl.when((band > 0) & (t != 1))
    def _():
        halo(1).start()

    loads[1].wait()
    project(1)
    send_z(0).wait_recv()
    for d in (1, 3, 2):
        send_x(d).start()
    loads[2].wait()
    project(2)

    lane = lax.broadcasted_iota(jnp.int32, (BLOCK, 128), 1)

    def give(unit, part, chip, core, slot, column):
        return pltpu.make_async_remote_copy(
            src_ref=att.at[rows_at(unit * WIDE + part * HALF, HALF), :],
            dst_ref=rcv.at[:, pl.ds(pl.multiple_of(column * 128, 128), 128)],
            send_sem=give_send.at[slot],
            recv_sem=give_recv.at[column],
            device_id={"head": chip * 2 + core},
            device_id_type=MESH,
        )

    def block(unit, chip, i, q_first, kv_first):
        local = chip * REACH + i
        att[rows_at(unit * WIDE + i * BLOCK, BLOCK), :] = attend_block(
            qs[rows_at(q_first + i * BLOCK, BLOCK), :],
            key_start[local] - (band * 4 * REACH + local - REACH),
            key_count[local],
            kv,
            kv_first + i * BLOCK,
            lane,
        )

    for i in range(7):
        block(0, t_a, i, t_a * WIDE, t_a * WIDE)
        if i == 1:
            for d in (1, 3, 2):
                recv_x(d).wait_recv()
            for d in (1, 3, 2):
                send_y(d).start()
        if i == 3:
            give(0, 0, t_a, 0, 0, head).start()
    give(0, 1, t_a, 1, 1, head).start()

    @pl.when((band > 0) & (t != 2))
    def _():
        halo(0).wait_recv()

    @pl.when((band < bands - 1) & (t != 1))
    def _():
        halo(1).wait_recv()

    for i in range(7):
        block(1, t_b, i, t_b * WIDE, t_b * WIDE)
        if i == 3:
            give(1, 0, t_b, 0, 2, head).start()
    give(1, 1, t_b, 1, 3, head).start()

    for d in (1, 3, 2):
        recv_y(d).wait_recv()
    send_z(1).wait_recv()
    inner = ((t + 1) // 2) % 2
    edge = 2 * (t // 2)
    project_far(t_b, (9 - inner * (3 - edge)) * WIDE)

    @pl.when((t == 0) & (band < bands - 1))
    def _():
        far_halo(0).start()

    @pl.when((t == 3) & (band > 0))
    def _():
        far_halo(1).start()

    project_far(t_a, (8 - edge) * WIDE)
    project_far(t, 7 * WIDE)

    def far_queries(s, carry):
        raw = jnp.dot(xv[rows_at(t * WIDE + s * STEP, STEP), :], wf[:, :128], preferred_element_type=F32)
        put_q(raw, gf, 4 * WIDE + s * STEP)
        return carry

    lax.fori_loop(0, WIDE // STEP, far_queries, 0)

    def keep(unit, column, sem):
        return pltpu.make_async_copy(
            att.at[rows_at(unit * WIDE + c * HALF, HALF), :],
            rcv.at[:, pl.ds(pl.multiple_of(column * 128, 128), 128)],
            keep_sem.at[sem],
        )

    for k in range(7):
        block(2, t, (k + 3 * (1 - c)) % 7, t * WIDE, t * WIDE)
        if k == 3:
            give(2, 1 - c, t, 1 - c, 4, head).start()
    keep(2, head, 0).start()

    hi = t // 2

    def part(k, count, base, skip):
        i = k + hi * (6 - 2 * k)
        local = t * REACH + i
        return i, attend_part(
            qs[rows_at(4 * WIDE + i * BLOCK, BLOCK), :],
            key_start[local] - (band * 4 * REACH + local - REACH) - skip,
            key_count[local],
            kv,
            6 * WIDE + base * BLOCK,
            lane,
            count,
        )

    for k in range(7):
        _, sums = part(k, 8 + k, 7 * (1 - hi) + hi * (6 - k), (1 - hi) * (7 - k))
        acc[pl.ds(k * 256, 256), :] = sums

    load_ow.wait()
    load_res.wait()
    keep(2, head, 0).wait()

    def arrive(column):
        pltpu.make_async_remote_copy(
            src_ref=att.at[pl.ds(0, HALF), :],
            dst_ref=rcv.at[:, pl.ds(pl.multiple_of(column * 128, 128), 128)],
            send_sem=give_send.at[0],
            recv_sem=give_recv.at[column],
            device_id={"head": t * 2 + 1 - c},
            device_id_type=MESH,
        ).wait_recv()

    def out_part(chip, r):
        columns = pl.ds(pl.multiple_of(chip * 256, 256), 256)
        return jnp.dot(rcv[pl.ds(r, 224), columns], ow[columns, :], preferred_element_type=F32)

    def edge_part(k):
        i, sums = part(k, 7 - k, (1 - hi) * k + 14 * hi, hi * (8 + k))
        sums = sums + acc[pl.ds(k * 256, 256), :]
        mixed = sums[:, :128] * (1.0 / sums[:, 128:])
        att[rows_at(3 * WIDE + i * BLOCK, BLOCK), :] = jnp.where(lane < 64, mixed[:BLOCK], mixed[BLOCK:]).astype(BF16)

    def edges(ks):
        for n, k in enumerate(ks):
            edge_part(k)
            if n == 3:
                give(3, 1 - c, t, 1 - c, 5, far).start()

    def first_parts():
        up = (t + 1) % 4
        down = (t + 3) % 4
        for column in (t * 2 + 1 - c, up * 2, up * 2 + 1, down * 2, down * 2 + 1):
            arrive(column)
        for r in range(0, HALF, 224):
            base = res[pl.ds(r, 224), :].astype(F32)
            total[pl.ds(r, 224), :] = base + (out_part(t, r) + out_part(up, r) + out_part(down, r))

    outer = (t == 0) | (t == 3)

    @pl.when(outer)
    def _():
        first_parts()

    @pl.when((t == 0) & (band > 0))
    def _():
        far_halo(0).wait_recv()

    @pl.when((t == 3) & (band < bands - 1))
    def _():
        far_halo(1).wait_recv()

    @pl.when((c + hi) % 2 == 1)
    def _():
        edges((0, 1, 2, 3, 4, 5, 6))

    @pl.when((c + hi) % 2 == 0)
    def _():
        edges((6, 5, 4, 3, 2, 1, 0))

    keep(3, far, 1).start()

    @pl.when((t == 1) | (t == 2))
    def _():
        first_parts()

    keep(3, far, 1).wait()
    arrive(t_op * 2 + 1 - c)
    for r in range(0, HALF, 224):
        out[pl.ds(r, 224), :] = (total[pl.ds(r, 224), :] + out_part(t_op, r)).astype(BF16)
    for slot in range(4):
        chip = (t_a, t_b)[slot // 2]
        give(slot // 2, slot % 2, chip, slot % 2, slot, head).wait_send()
    give(2, 1 - c, t, 1 - c, 4, head).wait_send()
    give(3, 1 - c, t, 1 - c, 5, far).wait_send()
    send_z(0).wait_send()
    send_z(1).wait_send()
    for d in (1, 2, 3):
        send_x(d).wait_send()
        send_y(d).wait_send()

    @pl.when((band < bands - 1) & (t != 2))
    def _():
        halo(0).wait_send()

    @pl.when((band > 0) & (t != 1))
    def _():
        halo(1).wait_send()

    @pl.when((t == 0) & (band < bands - 1))
    def _():
        far_halo(0).wait_send()

    @pl.when((t == 3) & (band > 0))
    def _():
        far_halo(1).wait_send()


def on_device(tokens, ln_gain, qkv_weight, qk_gain, out_weight, key_start, key_count):
    rows, features = tokens.shape
    columns = qk_gain.shape[1] * qk_gain.shape[2]
    weight = jnp.transpose(qkv_weight, (1, 0, 2))
    whole = pl.BlockSpec(memory_space=pltpu.VMEM)
    scalars = pl.BlockSpec(memory_space=pltpu.SMEM)
    far = pl.BlockSpec(memory_space=pl.ANY)
    return pl.pallas_call(
        layer,
        out_shape=jax.ShapeDtypeStruct((HALF, features), BF16),
        in_specs=[far, whole, far, whole, far, scalars, scalars],
        out_specs=whole,
        scratch_shapes=[
            pltpu.VMEM((rows, features), BF16),
            pltpu.VMEM((features, 3 * columns), BF16),
            pltpu.VMEM((features, 3 * columns), BF16),
            pltpu.VMEM((8, 128), F32),
            pltpu.VMEM((8, 128), F32),
            pltpu.VMEM((features, features), BF16),
            pltpu.VMEM((10 * WIDE, 256), BF16),
            pltpu.VMEM((5 * WIDE, 128), BF16),
            pltpu.VMEM((REACH * 256, 256), F32),
            pltpu.VMEM((HALF, features), F32),
            pltpu.VMEM((4 * WIDE, 128), BF16),
            pltpu.VMEM((HALF, features), BF16),
            pltpu.VMEM((HALF, features), BF16),
            pltpu.SemaphoreType.DMA((4,)),
            pltpu.SemaphoreType.DMA((5,)),
            pltpu.SemaphoreType.DMA((3,)),
            pltpu.SemaphoreType.DMA((3,)),
            pltpu.SemaphoreType.DMA((6,)),
            pltpu.SemaphoreType.DMA((8,)),
            pltpu.SemaphoreType.DMA((2,)),
            pltpu.SemaphoreType.DMA((2,)),
            pltpu.SemaphoreType.DMA((2,)),
            pltpu.SemaphoreType.DMA((6,)),
            pltpu.SemaphoreType.DMA((6,)),
        ],
        compiler_params=pltpu.CompilerParams(
            vmem_limit_bytes=56 << 20, collective_id=0, has_side_effects=True
        ),
        name="layer",
    )(tokens, ln_gain.reshape(1, features), weight, qk_gain, out_weight, key_start, key_count)


def solution(mesh):
    placed = (
        P(("member", "band"), None),
        P(),
        P(None, None, "head"),
        P(None, "head", None),
        P(),
        P("band"),
        P("band"),
    )
    return jax.shard_map(
        on_device,
        mesh=mesh,
        in_specs=placed,
        out_specs=P(("member", "band", "head"), None),
        check_vma=False,
    )
```
